256 devices in a mesh: dp: 8 (over y, core), vocab: 32 (over z, x).
Axes of the slice: x: 4, y: 4, z: 8, core: 2. Of those that a mesh axis runs over, the one named last changes fastest.
Arguments:
- token_grads: bfloat16 [524288, 1024], P(('dp', 'vocab')), may hold values from -6 to 6
- token_ids: int32 [524288], P(('dp', 'vocab')), may hold values from 0 to 125183, as said below
Outputs:
- delta_grad: float32 [125184, 1024], P('vocab', 'dp')
The draws below stay inside these ranges and needn't reach their ends.
Inputs may be any that keep to these rules, and one draw needn't show every extreme that they name: `token_ids`: ids are skewed toward a few common ones within each shard of 3912 consecutive ids. Among the rows of one device at most 96 ids lie in one shard, and exactly 96 lie in one shard, the same shard for every device of a data group.
All inputs are finite; a program needn't handle non-finite values.
Results may differ from the reference program's by a relative error of at most 0.0003.
Values may be sent and summed in bfloat16 or wider, within the bound.
A program may use at most 128 MiB of HBM per device.

```python
import jax
import jax.numpy as jnp
from jax import lax

D = 1024
VSH = 3912
ROWS_DEV = 2048
GROUPS = 8
SHARDS = 32
CAP = 96
ROWS = 524288


def draw_token_ids(key, part):
    key = jax.random.fold_in(key, 5)
    keys = jax.random.split(key, 5)
    hot = jax.random.randint(keys[0], (GROUPS, 1, 1), 0, SHARDS)
    offset = jax.random.randint(keys[1], (GROUPS, SHARDS, 1), 0, SHARDS - 1)
    place = jnp.arange(ROWS_DEV)[None, None, :]
    other = (hot + 1 + (place - CAP + offset) % (SHARDS - 1)) % SHARDS
    owner = jnp.where(place < CAP, hot, other)
    owner = jnp.broadcast_to(owner, (GROUPS, SHARDS, ROWS_DEV))
    perm_keys = jax.random.split(keys[2], GROUPS * SHARDS)
    order = jax.vmap(lambda k: jax.random.permutation(k, ROWS_DEV))(perm_keys).reshape(GROUPS, SHARDS, ROWS_DEV)
    owner = jnp.take_along_axis(owner, order, axis=2)
    base = jax.random.randint(keys[3], (GROUPS, SHARDS, ROWS_DEV), 0, VSH)
    spread = jax.random.randint(keys[4], (GROUPS, SHARDS, ROWS_DEV), 1, VSH + 1)
    local = base % spread
    return (owner * VSH + local).reshape(-1).astype(jnp.int32)


def shard_levels(stream_key, extent, pieces, smallest, high):
    level, own = 1.0, jax.random.fold_in(stream_key, 6)
    for dim, parts in pieces:
        heights = jnp.exp(jax.random.uniform(jax.random.fold_in(own, dim), (parts,), jnp.float32, smallest / len(pieces), high / len(pieces)))
        level = level * jnp.repeat(heights, extent[dim] // parts).reshape([-1 if axis == dim else 1 for axis in range(len(extent))])
    return level


def noise(rng, shape, deviation, reach, cuts=(), dtype=jnp.bfloat16):
    drawn = deviation * jax.random.normal(rng, shape, jnp.float32)
    if cuts:
        drawn = drawn * shard_levels(rng, shape, cuts, -0.22, 0.18)
    return jnp.clip(drawn, -reach, reach).astype(dtype)


def setup_inputs(seed: int = 0) -> dict:
    arg_keys = jax.random.split(jax.random.key(seed), 3)
    return {
        "token_grads": noise(arg_keys[0], (ROWS, D), 1.0, 6.0, ((0, 256),)),
        "token_ids": draw_token_ids(jax.random.fold_in(arg_keys[2], 71), 0),
    }


def reference(token_grads, token_ids):
    grads = token_grads.reshape(GROUPS, -1, D)
    ids = token_ids.reshape(GROUPS, -1)

    def step(total, item):
        rows, idx = item
        part = jax.ops.segment_sum(rows.astype(jnp.float32), idx, num_segments=VSH * SHARDS)
        return total + part, None

    total, _ = lax.scan(step, jnp.zeros((VSH * SHARDS, D), jnp.float32), (grads, ids))
    return total
```

```python
import functools

import jax
import jax.numpy as jnp
from jax import lax
from jax.experimental import pallas as pl
from jax.experimental.pallas import tpu as pltpu
from jax.sharding import PartitionSpec as P

MESH = pl.DeviceIdType.MESH
VSH = 3912
SHARDS = 32
CAP = 96
ROWS = 2048
CHUNK = 784
CHUNKS = 5
QUARTER = 256
HALF = 128
BATCHES = 8
PEERS = 128


def place():
    dp, vocab = lax.axis_index("dp"), lax.axis_index("vocab")
    return dp // 2, dp % 2, vocab // 4, vocab % 4


def target(b, i, dy):
    y, c, z, x = place()
    to_z = (z + 2 * i + b % 2) % 8
    to_x = (x + i + b // 2) % 4
    to_y = (y + dy) % 4
    return (to_y * 2 + c, to_z * 4 + to_x), to_y, to_z * 4 + to_x


def rank_rows(ids_ref, rank, parts):
    ids = ids_ref[...]
    first = lax.broadcasted_iota(jnp.int32, (SHARDS, 1), 0) * VSH
    local = ids - first
    inside = (local >= 0) & (local < VSH)
    mine = jnp.sum(jnp.where(inside, local, 0), axis=0, keepdims=True)
    row = lax.broadcasted_iota(jnp.int32, (16, ROWS), 0)
    hi, lo = mine >> 6, mine & 63
    parts[...] = jnp.where(row == 0, hi, jnp.where(row == 1, lo, 0)).astype(jnp.float32).astype(jnp.bfloat16)
    block = 256
    before = lax.broadcasted_iota(jnp.int32, (block, block), 0) < lax.broadcasted_iota(jnp.int32, (block, block), 1)
    before = jnp.where(before, 1.0, 0.0).astype(jnp.bfloat16)
    carry = jnp.zeros((SHARDS, 1), jnp.float32)
    marks = jnp.where(inside, 1.0, 0.0)
    for k in range(ROWS // block):
        m = marks[:, k * block : (k + 1) * block]
        count = jnp.dot(m.astype(jnp.bfloat16), before, preferred_element_type=jnp.float32) + carry
        rank[:, k * block : (k + 1) * block] = jnp.where(m > 0.5, count, -1.0).astype(jnp.int32)
        carry = carry + jnp.sum(m, axis=1, keepdims=True)


def kernel(cap, ids_ref, grads_ref, out_ref, rank, parts, send, send_ids, recv, recv_ids, acc, other, ssem, isem, rsem, jsem, psem, qsem):
    y, c, z, x = place()
    partner = (y * 2 + 1 - c, z * 4 + x)
    barrier = pltpu.get_barrier_semaphore()

    def greet(j, _):
        peer, _, _ = target(j // 16, j // 4 % 4, j % 4)
        pl.semaphore_signal(barrier, inc=1, device_id=peer, device_id_type=MESH)
        return 0

    lax.fori_loop(1, PEERS, greet, 0)
    pl.semaphore_signal(barrier, inc=1, device_id=partner, device_id_type=MESH)
    rank_rows(ids_ref, rank, parts)
    send_ids[...] = jnp.zeros_like(send_ids)
    pl.semaphore_wait(barrier, PEERS)

    def rows_copy(b, i, dy):
        peer, _, _ = target(b, i, dy)
        j = b * 16 + i * 4 + dy
        return pltpu.make_async_remote_copy(send.at[j], recv.at[j], ssem.at[j], rsem.at[j], device_id=peer, device_id_type=MESH)

    def ids_copy(b, i, dy):
        peer, _, _ = target(b, i, dy)
        j = b * 16 + i * 4 + dy
        return pltpu.make_async_remote_copy(
            send_ids.at[b * 4 + i], recv_ids.at[j], isem.at[j], jsem.at[j], device_id=peer, device_id_type=MESH
        )

    own_rows = pltpu.make_async_copy(send.at[0], recv.at[0], rsem.at[0])
    own_ids = pltpu.make_async_copy(send_ids.at[0], recv_ids.at[0], jsem.at[0])

    def pack(b, _):
        picks = []
        slot = lax.broadcasted_iota(jnp.int32, (cap, ROWS), 0)
        for i in range(4):
            _, _, shard = target(b, i, 0)
            pick = jnp.where(rank[pl.ds(shard, 1), :] == slot, 1.0, 0.0).astype(jnp.bfloat16)
            pair = lax.dot_general(parts[...], pick, (((1,), (1,)), ((), ())), preferred_element_type=jnp.float32)
            local = (pair[0:1] * 64.0 + pair[1:2]).astype(jnp.int32)
            send_ids[b * 4 + i, :, 0:cap] = local
            picks.append(pick)
        picks = jnp.concatenate(picks, axis=0)
        for dy in range(4):
            _, to_y, _ = target(b, 0, dy)
            cols = pl.ds(pl.multiple_of(to_y * QUARTER, QUARTER), QUARTER)
            packed = jnp.dot(picks, grads_ref[:, cols], preferred_element_type=jnp.float32).astype(jnp.bfloat16)
            for i in range(4):
                send[b * 16 + i * 4 + dy] = packed[i * cap : (i + 1) * cap]
                if i == 0 and dy == 0:

                    @pl.when(b == 0)
                    def _():
                        own_rows.start()
                        own_ids.start()

                    @pl.when(b > 0)
                    def _():
                        rows_copy(b, 0, 0).start()
                        ids_copy(b, 0, 0).start()
                else:
                    rows_copy(b, i, dy).start()
                    ids_copy(b, i, dy).start()
        return 0

    lax.fori_loop(0, BATCHES, pack, 0)

    def chunk_sum(b, t, ids):
        start = pl.multiple_of(t * CHUNK, 16)
        row = lax.broadcasted_iota(jnp.int32, (CHUNK, 16 * cap), 0)
        hit = jnp.where(row == ids - start, 1.0, 0.0).astype(jnp.bfloat16)
        return start, jnp.dot(hit, recv[pl.ds(b * 16, 16)].reshape(16 * cap, QUARTER), preferred_element_type=jnp.float32)

    def arrive(b):
        def wait(k, _):
            rows_copy(b, k // 4, k % 4).wait_recv()
            ids_copy(b, k // 4, k % 4).wait_recv()
            return 0

        if isinstance(b, int) and b == 0:
            own_rows.wait()
            own_ids.wait()
            lax.fori_loop(1, 16, wait, 0)
        else:
            lax.fori_loop(0, 16, wait, 0)
        return jnp.concatenate([recv_ids[b * 16 + k][:, 0:cap] for k in range(16)], axis=1)

    def exchange(t):
        rows = pl.ds(pl.multiple_of(t * CHUNK, 16), CHUNK)
        return pltpu.make_async_remote_copy(
            acc.at[1 - c, rows], other.at[rows], psem.at[t], qsem.at[t], device_id=partner, device_id_type=MESH
        )

    def add(b, t, ids, fresh=False):
        start, part = chunk_sum(b, t, ids)
        rows = pl.ds(start, CHUNK)
        if fresh:
            acc[0, rows] = part[:, :HALF]
            acc[1, rows] = part[:, HALF:]
        else:
            acc[0, rows] += part[:, :HALF]
            acc[1, rows] += part[:, HALF:]

    def first(t, ids):
        add(0, t, ids, fresh=True)
        return ids

    def later(b, _):
        ids = arrive(b)

        def step(t, ids):
            add(b, t, ids)
            return ids

        lax.fori_loop(0, CHUNKS, step, ids)
        return 0

    def last(t, ids):
        add(BATCHES - 1, t, ids)
        exchange(t).start()
        return ids

    lax.fori_loop(0, CHUNKS, first, arrive(0))
    lax.fori_loop(1, BATCHES - 1, later, 0)
    lax.fori_loop(0, CHUNKS, last, arrive(BATCHES - 1))

    for t in range(CHUNKS):
        exchange(t).wait()
        n = min(CHUNK, VSH - t * CHUNK)
        out_ref[t * CHUNK : t * CHUNK + n] = acc[c, t * CHUNK : t * CHUNK + n] + other[t * CHUNK : t * CHUNK + n]

    def drain(j, _):
        rows_copy(j // 16, j // 4 % 4, j % 4).wait_send()
        ids_copy(j // 16, j // 4 % 4, j % 4).wait_send()
        return 0

    lax.fori_loop(1, PEERS, drain, 0)


def body(token_grads, token_ids):
    cap = CAP
    return pl.pallas_call(
        functools.partial(kernel, cap),
        out_shape=jax.ShapeDtypeStruct((VSH, HALF), jnp.float32),
        in_specs=[pl.BlockSpec(memory_space=pltpu.VMEM)] * 2,
        out_specs=pl.BlockSpec(memory_space=pltpu.VMEM),
        scratch_shapes=[
            pltpu.VMEM((SHARDS, ROWS), jnp.int32),
            pltpu.VMEM((16, ROWS), jnp.bfloat16),
            pltpu.VMEM((PEERS, cap, QUARTER), jnp.bfloat16),
            pltpu.VMEM((SHARDS, 1, 128), jnp.int32),
            pltpu.VMEM((PEERS, cap, QUARTER), jnp.bfloat16),
            pltpu.VMEM((PEERS, 1, 128), jnp.int32),
            pltpu.VMEM((2, CHUNK * CHUNKS, HALF), jnp.float32),
            pltpu.VMEM((CHUNK * CHUNKS, HALF), jnp.float32),
            pltpu.SemaphoreType.DMA((PEERS,)),
            pltpu.SemaphoreType.DMA((PEERS,)),
            pltpu.SemaphoreType.DMA((PEERS,)),
            pltpu.SemaphoreType.DMA((PEERS,)),
            pltpu.SemaphoreType.DMA((CHUNKS,)),
            pltpu.SemaphoreType.DMA((CHUNKS,)),
        ],
        compiler_params=pltpu.CompilerParams(collective_id=0, has_side_effects=True, vmem_limit_bytes=56 << 20),
        name="delta_grad",
    )(token_ids.reshape(1, ROWS), token_grads)


def solution(mesh):
    return jax.shard_map(
        body,
        mesh=mesh,
        in_specs=(P(("dp", "vocab"), None), P(("dp", "vocab"))),
        out_specs=P("vocab", "dp"),
        check_vma=False,
    )
```

```python
import functools

import jax
import jax.numpy as jnp
from jax import lax
from jax.experimental import pallas as pl
from jax.experimental.pallas import tpu as pltpu
from jax.sharding import PartitionSpec as P

MESH = pl.DeviceIdType.MESH
VSH = 3912
SHARDS = 32
ROWS = 2048
DIRECT = 64
REST = 32
EXTRA = 32
CHUNK = 784
CHUNKS = 5
QUARTER = 256
HALF = 128
BATCHES = 8
PEERS = 128
NEAR = 32
PARTS = 2
THROTTLE = 8


def place():
    dp, vocab = lax.axis_index("dp"), lax.axis_index("vocab")
    return dp // 2, dp % 2, vocab // 4, vocab % 4


def offset(b, i):
    return 2 * i + b % 2, b // 2


def target(b, i, dy):
    y, c, z, x = place()
    dz, dx = offset(b, i)
    to_z, to_x, to_y = (z + dz) % 8, (x + dx) % 4, (y + dy) % 4
    return (to_y * 2 + c, to_z * 4 + to_x), to_y, to_z * 4 + to_x


def running(marks, before, carry):
    count = jnp.dot(marks.astype(jnp.bfloat16), before, preferred_element_type=jnp.float32) + carry
    return count, carry + jnp.sum(marks, axis=1, keepdims=True)


def rank_rows(ids_ref, rank, extra, parts):
    ids = ids_ref[...]
    first = lax.broadcasted_iota(jnp.int32, (SHARDS, 1), 0) * VSH
    local = ids - first
    marks = jnp.where((local >= 0) & (local < VSH), 1.0, 0.0)
    row = lax.broadcasted_iota(jnp.int32, (16, ROWS), 0)
    split = jnp.where(row == 0, ids >> 12, jnp.where(row == 1, (ids >> 6) & 63, jnp.where(row == 2, ids & 63, 0)))
    parts[...] = split.astype(jnp.float32).astype(jnp.bfloat16)
    block = 256
    before = lax.broadcasted_iota(jnp.int32, (block, block), 0) < lax.broadcasted_iota(jnp.int32, (block, block), 1)
    before = jnp.where(before, 1.0, 0.0).astype(jnp.bfloat16)
    carry = jnp.zeros((SHARDS, 1), jnp.float32)
    total = jnp.zeros((16, 1), jnp.float32)
    for k in range(ROWS // block):
        m = marks[:, k * block : (k + 1) * block]
        count, carry = running(m, before, carry)
        count = jnp.where(m > 0.5, count, -1.0)
        rank[:, k * block : (k + 1) * block] = count.astype(jnp.int32)
        over = jnp.sum(jnp.where(count >= DIRECT, 1.0, 0.0), axis=0, keepdims=True)
        over = jnp.broadcast_to(over, (16, block))
        place_of, total = running(over, before, total)
        place_of = jnp.where(over > 0.5, place_of, -1.0).astype(jnp.int32)
        extra[:, k * block : (k + 1) * block] = place_of[0:8]
    return total[0:1]


def kernel(main, cap, *refs):
    if main:
        (ids_ref, grads_hbm, out_ref, flag_ref), refs = refs[:4], refs[4:]
    else:
        (ids_ref, grads_hbm, sum_ref, out_ref), refs = refs[:4], refs[4:]
    grads_ref, lsem, rank, extra, parts, send, send_ids, recv, recv_ids, acc, other, ssem, isem, rsem, jsem, psem, qsem = refs[:17]
    if main:
        far_send, far, fs, fr, gs, gr = refs[17:]
    y, c, z, x = place()
    partner = (y * 2 + 1 - c, z * 4 + x)
    shard = z * 4 + x
    barrier = pltpu.get_barrier_semaphore()

    load = pltpu.make_async_copy(grads_hbm, grads_ref, lsem)
    load.start()
    planes = [(z + dz) % 8 * 4 for dz in range(8)]
    lines = [(x + dx) % 4 for dx in range(4)]
    groups = [(y + dy) % 4 * 2 + c for dy in range(4)]
    for j in range(1, PEERS):
        dz, dx, dy = j // 16, j // 4 % 4, j % 4
        peer = (groups[dy], planes[dz] + lines[dx])
        pl.semaphore_signal(barrier, inc=1, device_id=peer, device_id_type=MESH)
    pl.semaphore_signal(barrier, inc=1, device_id=partner, device_id_type=MESH)
    total = rank_rows(ids_ref, rank, extra, parts)
    send_ids[...] = jnp.zeros_like(send_ids)
    if main:
        spare = jnp.where(extra[0:1, :] >= 0, extra[0:1, :], EXTRA)
        pick_far = jnp.where(spare == lax.broadcasted_iota(jnp.int32, (EXTRA, ROWS), 0), 1.0, 0.0).astype(jnp.bfloat16)
    else:
        late = extra[0:1, :] >= EXTRA
        rank[...] = jnp.where(late & (rank[...] >= DIRECT), rank[...] - DIRECT, -1)
    def rows_copy(b, i, dy):
        peer, _, _ = target(b, i, dy)
        j = b * 16 + i * 4 + dy
        return pltpu.make_async_remote_copy(send.at[j], recv.at[j], ssem.at[j], rsem.at[j], device_id=peer, device_id_type=MESH)

    def ids_copy(b, i, dy):
        peer, _, _ = target(b, i, dy)
        j = b * 16 + i * 4 + dy
        return pltpu.make_async_remote_copy(
            send_ids.at[b * 4 + i], recv_ids.at[j], isem.at[j], jsem.at[j], device_id=peer, device_id_type=MESH
        )

    def far_copy(j):
        peer, _, _ = target(j // 16, j // 4 % 4, j % 4)
        return pltpu.make_async_remote_copy(far_send.at[j % 4], far.at[0, j], fs.at[j], fr.at[j], device_id=peer, device_id_type=MESH)

    def onward(part, dx):
        n = NEAR // PARTS
        s = part * 3 + dx - 1
        return pltpu.make_async_remote_copy(
            far.at[0, pl.ds(part * n, n)],
            far.at[dx, pl.ds(part * n, n)],
            gs.at[s],
            gr.at[s],
            device_id=(y * 2 + c, z * 4 + (x + dx) % 4),
            device_id_type=MESH,
        )

    own_rows = pltpu.make_async_copy(send.at[0], recv.at[0], rsem.at[0])
    own_ids = pltpu.make_async_copy(send_ids.at[0], recv_ids.at[0], jsem.at[0])

    def ids_of(pick):
        three = lax.dot_general(parts[...], pick, (((1,), (1,)), ((), ())), preferred_element_type=jnp.float32)
        return (three[0:1] * 4096.0 + three[1:2] * 64.0 + three[2:3]).astype(jnp.int32)

    if main:
        far_ids = ids_of(pick_far)
        for k in range(SHARDS):
            send_ids[k, :, cap : cap + EXTRA] = far_ids
            send_ids[k, :, 127:128] = jnp.where(total > EXTRA, 1, 0)
        load.wait()
        for dy in range(4):
            _, to_y, _ = target(0, 0, dy)
            cols = pl.ds(pl.multiple_of(to_y * QUARTER, QUARTER), QUARTER)
            packed = jnp.dot(pick_far, grads_ref[:, cols], preferred_element_type=jnp.float32).astype(jnp.bfloat16)
            far_send[dy] = packed
        pl.semaphore_wait(barrier, PEERS)
        own_far = pltpu.make_async_copy(far_send.at[0], far.at[0, 0], fr.at[0])
        own_far.start()

        def send_far(j, _):
            far_copy(j).start()
            return 0

        lax.fori_loop(1, NEAR, send_far, 0)
    else:
        load.wait()
        pl.semaphore_wait(barrier, PEERS)

    def pack(b, _):
        if THROTTLE < BATCHES:

            @pl.when(b >= THROTTLE)
            def _():
                lax.fori_loop(jnp.where(b == THROTTLE, 1, 0), 16, lambda k, _: sent((b - THROTTLE) * 16 + k, 0), 0)

        picks = []
        slot = lax.broadcasted_iota(jnp.int32, (cap, ROWS), 0)
        for i in range(4):
            _, _, to_shard = target(b, i, 0)
            pick = jnp.where(rank[pl.ds(to_shard, 1), :] == slot, 1.0, 0.0).astype(jnp.bfloat16)
            send_ids[b * 4 + i, :, 0:cap] = ids_of(pick) - to_shard * VSH
            picks.append(pick)
        picks = jnp.concatenate(picks, axis=0)
        for dy in range(4):
            _, to_y, _ = target(b, 0, dy)
            cols = pl.ds(pl.multiple_of(to_y * QUARTER, QUARTER), QUARTER)
            packed = jnp.dot(picks, grads_ref[:, cols], preferred_element_type=jnp.float32).astype(jnp.bfloat16)
            for i in range(4):
                send[b * 16 + i * 4 + dy] = packed[i * cap : (i + 1) * cap]
                if i == 0 and dy == 0:

                    @pl.when(b == 0)
                    def _():
                        own_rows.start()
                        own_ids.start()

                    @pl.when(b > 0)
                    def _():
                        ids_copy(b, 0, 0).start()
                        rows_copy(b, 0, 0).start()
                else:
                    ids_copy(b, i, dy).start()
                    rows_copy(b, i, dy).start()
        return 0

    def sent(j, _):
        rows_copy(j // 16, j // 4 % 4, j % 4).wait_send()
        ids_copy(j // 16, j // 4 % 4, j % 4).wait_send()
        return 0

    def add(block, t, ids, fresh=False):
        start = pl.multiple_of(t * CHUNK, 16)
        row = lax.broadcasted_iota(jnp.int32, (CHUNK, block.shape[0]), 0)
        hit = jnp.where(row == ids - start, 1.0, 0.0).astype(jnp.bfloat16)
        part = jnp.dot(hit, block, preferred_element_type=jnp.float32)
        rows = pl.ds(start, CHUNK)
        if fresh:
            acc[0, rows] = part[:, :HALF]
            acc[1, rows] = part[:, HALF:]
        else:
            acc[0, rows] += part[:, :HALF]
            acc[1, rows] += part[:, HALF:]

    def rows_of(b):
        return recv[pl.ds(b * 16, 16)].reshape(16 * cap, QUARTER)

    def arrive(b, ids=True, rows=True):
        def wait(k, _):
            if rows:
                rows_copy(b, k // 4, k % 4).wait_recv()
            if ids:
                ids_copy(b, k // 4, k % 4).wait_recv()
            return 0

        if isinstance(b, int) and b == 0:
            own_rows.wait()
            own_ids.wait()
            lax.fori_loop(1, 16, wait, 0)
        else:
            lax.fori_loop(0, 16, wait, 0)

    def ids_of_batch(b):
        return jnp.concatenate([recv_ids[b * 16 + k][:, 0:cap] for k in range(16)], axis=1)

    def exchange(t):
        rows = pl.ds(pl.multiple_of(t * CHUNK, 16), CHUNK)
        return pltpu.make_async_remote_copy(
            acc.at[1 - c, rows], other.at[rows], psem.at[t], qsem.at[t], device_id=partner, device_id_type=MESH
        )

    def sweep(block, ids, fresh=False, then=None):
        def step(t, ids):
            add(block(), t, ids, fresh)
            if then is not None:
                then(t)
            return ids

        lax.fori_loop(0, CHUNKS, step, ids)

    def batch(b, _):
        arrive(b)
        sweep(lambda: rows_of(b), ids_of_batch(b))
        return 0

    def far_block(dx):
        ids = [recv_ids[dx * NEAR + k][:, cap : cap + EXTRA] for k in range(NEAR)]
        ids = jnp.concatenate(ids, axis=1) - shard * VSH
        sweep(lambda: far[dx].reshape(NEAR * EXTRA, QUARTER), ids)

    lax.fori_loop(0, BATCHES, pack, 0)
    arrive(0)
    sweep(lambda: rows_of(0), ids_of_batch(0), fresh=True)
    if main:
        for part in range(PARTS):
            if part == 0:
                own_far.wait()
            lax.fori_loop(max(1, part * NEAR // PARTS), (part + 1) * NEAR // PARTS, lambda j, _: far_copy(j).wait_recv() or 0, 0)
            for dx in (1, 2, 3):
                onward(part, dx).start()
        batch(1, 0)
        far_block(0)
        for dx in (1, 2, 3):
            lax.fori_loop(2 * dx, 2 * dx + 2 if dx < 3 else 7, batch, 0)
            for part in range(PARTS):
                onward(part, dx).wait_recv()
            if dx == 3:
                arrive(7, rows=False)
            far_block(dx)
        worst = functools.reduce(jnp.maximum, [recv_ids[j][:, 127:128] for j in range(PEERS)])
        mark = jnp.broadcast_to(worst.astype(jnp.float32), (8, HALF))

        def then(t):
            @pl.when(t == CHUNKS - 1)
            def _():
                acc[1 - c, VSH : VSH + 8] = mark

            exchange(t).start()

        arrive(7, ids=False)
        sweep(lambda: rows_of(7), ids_of_batch(7), then=then)
    else:
        lax.fori_loop(1, 7, batch, 0)
        arrive(7)
        sweep(lambda: rows_of(7), ids_of_batch(7), then=lambda t: exchange(t).start())

    for t in range(CHUNKS):
        exchange(t).wait()
        a, n = t * CHUNK, min(CHUNK, VSH - t * CHUNK)
        result = acc[c, a : a + n] + other[a : a + n]
        out_ref[a : a + n] = result if main else sum_ref[a : a + n] + result
    if main:
        flag_ref[...] = jnp.maximum(mark, other[VSH : VSH + 8]).astype(jnp.int32)
        for part in range(PARTS):
            for dx in (1, 2, 3):
                onward(part, dx).wait_send()
        lax.fori_loop(1, NEAR, lambda j, _: far_copy(j).wait_send() or 0, 0)
    lax.fori_loop(max(1, (BATCHES - THROTTLE) * 16), PEERS, sent, 0)


def call(main, cap, *operands):
    shape = jax.ShapeDtypeStruct((VSH, HALF), jnp.float32)
    dma = pltpu.SemaphoreType.DMA
    scratch = [
        pltpu.VMEM((ROWS, 4 * QUARTER), jnp.bfloat16),
        dma,
        pltpu.VMEM((SHARDS, ROWS), jnp.int32),
        pltpu.VMEM((8, ROWS), jnp.int32),
        pltpu.VMEM((16, ROWS), jnp.bfloat16),
        pltpu.VMEM((PEERS, cap, QUARTER), jnp.bfloat16),
        pltpu.VMEM((SHARDS, 1, 128), jnp.int32),
        pltpu.VMEM((PEERS, cap, QUARTER), jnp.bfloat16),
        pltpu.VMEM((PEERS, 1, 128), jnp.int32),
        pltpu.VMEM((2, CHUNK * CHUNKS, HALF), jnp.float32),
        pltpu.VMEM((CHUNK * CHUNKS, HALF), jnp.float32),
    ] + [dma((PEERS,))] * 4 + [dma((CHUNKS,))] * 2
    if main:
        scratch += [
            pltpu.VMEM((4, EXTRA, QUARTER), jnp.bfloat16),
            pltpu.VMEM((4, NEAR, EXTRA, QUARTER), jnp.bfloat16),
        ] + [dma((NEAR,))] * 2 + [dma((3 * PARTS,))] * 2
    return pl.pallas_call(
        functools.partial(kernel, main, cap),
        out_shape=(shape, jax.ShapeDtypeStruct((8, HALF), jnp.int32)) if main else shape,
        in_specs=[pl.BlockSpec(memory_space=pl.ANY if k == 1 else pltpu.VMEM) for k in range(len(operands))],
        out_specs=[pl.BlockSpec(memory_space=pltpu.VMEM)] * 2 if main else pl.BlockSpec(memory_space=pltpu.VMEM),
        scratch_shapes=scratch,
        compiler_params=pltpu.CompilerParams(
            collective_id=0 if main else 1, has_side_effects=True, vmem_limit_bytes=56 << 20
        ),
        name="direct_rows" if main else "rest_rows",
    )(*operands)


def body(token_grads, token_ids):
    ids = token_ids.reshape(1, ROWS)
    sums, flag = call(True, DIRECT, ids, token_grads)
    return lax.cond(
        flag[0, 0] > 0,
        lambda ids, grads, sums: call(False, REST, ids, grads, sums),
        lambda ids, grads, sums: sums,
        ids,
        token_grads,
        sums,
    )


def solution(mesh):
    return jax.shard_map(
        body,
        mesh=mesh,
        in_specs=(P(("dp", "vocab"), None), P(("dp", "vocab"))),
        out_specs=P("vocab", "dp"),
        check_vma=False,
    )
```

```python
import functools

import jax
import jax.numpy as jnp
from jax import lax
from jax.experimental import pallas as pl
from jax.experimental.pallas import tpu as pltpu
from jax.sharding import PartitionSpec as P

MESH = pl.DeviceIdType.MESH
VSH = 3912
SHARDS = 32
ROWS = 2048
DIRECT = 64
REST = 32
EXTRA = 32
CHUNK = 784
CHUNKS = 5
QUARTER = 256
HALF = 128
BATCHES = 8
PEERS = 128
BLOCKS = 32
ORDER = (0, 3, 5, 1, 6, 4, 7, 2)
HOPS = ((0, 1, 1), (5, 6, 1), (3, 4, 1), (0, 7, 7), (3, 2, 7), (5, 4, 7))


def place():
    dp, vocab = lax.axis_index("dp"), lax.axis_index("vocab")
    return dp // 2, dp % 2, vocab // 4, vocab % 4


def offset(b, i):
    return 2 * i + b % 2, b // 2


def target(b, i, dy):
    y, c, z, x = place()
    dz, dx = offset(b, i)
    to_z, to_x, to_y = (z + dz) % 8, (x + dx) % 4, (y + dy) % 4
    return (to_y * 2 + c, to_z * 4 + to_x), to_y, to_z * 4 + to_x


def running(marks, before, carry):
    count = jnp.dot(marks.astype(jnp.bfloat16), before, preferred_element_type=jnp.float32) + carry
    return count, carry + jnp.sum(marks, axis=1, keepdims=True)


def rank_rows(ids_ref, rank, extra, parts):
    ids = ids_ref[...]
    first = lax.broadcasted_iota(jnp.int32, (SHARDS, 1), 0) * VSH
    local = ids - first
    marks = jnp.where((local >= 0) & (local < VSH), 1.0, 0.0)
    row = lax.broadcasted_iota(jnp.int32, (16, ROWS), 0)
    split = jnp.where(row == 0, ids >> 12, jnp.where(row == 1, (ids >> 6) & 63, jnp.where(row == 2, ids & 63, 0)))
    parts[...] = split.astype(jnp.float32).astype(jnp.bfloat16)
    block = 256
    before = lax.broadcasted_iota(jnp.int32, (block, block), 0) < lax.broadcasted_iota(jnp.int32, (block, block), 1)
    before = jnp.where(before, 1.0, 0.0).astype(jnp.bfloat16)
    carry = jnp.zeros((SHARDS, 1), jnp.float32)
    total = jnp.zeros((16, 1), jnp.float32)
    for k in range(ROWS // block):
        m = marks[:, k * block : (k + 1) * block]
        count, carry = running(m, before, carry)
        count = jnp.where(m > 0.5, count, -1.0)
        rank[:, k * block : (k + 1) * block] = count.astype(jnp.int32)
        over = jnp.sum(jnp.where(count >= DIRECT, 1.0, 0.0), axis=0, keepdims=True)
        over = jnp.broadcast_to(over, (16, block))
        place_of, total = running(over, before, total)
        place_of = jnp.where(over > 0.5, place_of, -1.0).astype(jnp.int32)
        extra[:, k * block : (k + 1) * block] = place_of[0:8]
    return total[0:1]


def kernel(main, cap, *refs):
    if main:
        (ids_ref, grads_hbm, out_hbm, flag_ref), refs = refs[:4], refs[4:]
    else:
        (ids_ref, grads_hbm, sum_ref, out_hbm), refs = refs[:4], refs[4:]
    grads_ref, lsem, rank, extra, parts, send, send_ids, recv, recv_ids, acc, other, ssem, isem, rsem, jsem, psem, qsem, osem, own = refs[:19]
    if main:
        far_send, far, fs, fr, zs, zr, gs, gr = refs[19:]
    y, c, z, x = place()
    partner = (y * 2 + 1 - c, z * 4 + x)
    shard = z * 4 + x
    barrier = pltpu.get_barrier_semaphore()

    load = pltpu.make_async_copy(grads_hbm, grads_ref, lsem)
    load.start()
    planes = [(z + dz) % 8 * 4 for dz in range(8)]
    lines = [(x + dx) % 4 for dx in range(4)]
    groups = [(y + dy) % 4 * 2 + c for dy in range(4)]
    for j in range(1, PEERS):
        dz, dx, dy = j // 16, j // 4 % 4, j % 4
        peer = (groups[dy], planes[dz] + lines[dx])
        pl.semaphore_signal(barrier, inc=1, device_id=peer, device_id_type=MESH)
    pl.semaphore_signal(barrier, inc=1, device_id=partner, device_id_type=MESH)
    total = rank_rows(ids_ref, rank, extra, parts)
    send_ids[...] = jnp.zeros_like(send_ids)
    if main:
        spare = jnp.where(extra[0:1, :] >= 0, extra[0:1, :], EXTRA)
        pick_far = jnp.where(spare == lax.broadcasted_iota(jnp.int32, (EXTRA, ROWS), 0), 1.0, 0.0).astype(jnp.bfloat16)
    else:
        late = extra[0:1, :] >= EXTRA
        rank[...] = jnp.where(late & (rank[...] >= DIRECT), rank[...] - DIRECT, -1)
    def slot_of(b, i):
        return b + jnp.where(b == BATCHES - 1, i // 2, 0)

    def settle(ref, start, count, sem):
        span = ref.at[pl.ds(start, count)]
        pltpu.make_async_copy(span, span, sem).wait()

    def rows_copy(b, i, dy):
        peer, _, _ = target(b, i, dy)
        j = b * 16 + i * 4 + dy
        return pltpu.make_async_remote_copy(send.at[j], recv.at[j], ssem.at[b], rsem.at[slot_of(b, i)], device_id=peer, device_id_type=MESH)

    def ids_copy(b, i, dy):
        peer, _, _ = target(b, i, dy)
        j = b * 16 + i * 4 + dy
        return pltpu.make_async_remote_copy(
            send_ids.at[b * 4 + i], recv_ids.at[j], isem.at[b], jsem.at[b], device_id=peer, device_id_type=MESH
        )

    def far_copy(p, dy):
        source = far_send.at[dy - 1] if dy else far.at[0, 0]
        peer = ((y + dy) % 4 * 2 + c, (z + ORDER[p]) % 8 * 4 + x)
        return pltpu.make_async_remote_copy(source, far.at[0, p * 4 + dy], fs, fr, device_id=peer, device_id_type=MESH)

    def far_hop(k):
        took, gives, dz = HOPS[k]
        first, count = (0, 4) if gives != 4 else (0, 2) if dz == 1 else (2, 2)
        return pltpu.make_async_remote_copy(
            far.at[0, pl.ds(ORDER.index(took) * 4 + first, count)],
            far.at[0, pl.ds(ORDER.index(gives) * 4 + first, count)],
            zs.at[k],
            zr.at[k],
            device_id=(y * 2 + c, (z + dz) % 8 * 4 + x),
            device_id_type=MESH,
        )

    def onward(part, dx):
        span = pl.ds(0, 12) if part == 0 else pl.ds(12, 20)
        s = part * 3 + dx - 1
        return pltpu.make_async_remote_copy(
            far.at[0, span],
            far.at[dx, span],
            gs.at[s],
            gr.at[s],
            device_id=(y * 2 + c, z * 4 + (x + dx) % 4),
            device_id_type=MESH,
        )

    def forward():
        settle(far.at[0], 1, 11, fr)
        for k in range(len(HOPS)):
            far_hop(k).start()
        for dx in (1, 2, 3):
            onward(0, dx).start()

    own_rows = pltpu.make_async_copy(send.at[0], recv.at[0], own.at[0])
    own_ids = pltpu.make_async_copy(send_ids.at[0], recv_ids.at[0], own.at[1])

    def ids_by(pick):
        three = lax.dot_general(parts[...], pick, (((1,), (1,)), ((), ())), preferred_element_type=jnp.float32)
        return (three[0:1] * 4096.0 + three[1:2] * 64.0 + three[2:3]).astype(jnp.int32)

    if main:
        far_ids = ids_by(pick_far)
        for k in range(SHARDS):
            send_ids[k, :, cap : cap + EXTRA] = far_ids
            send_ids[k, :, 127:128] = jnp.where(total > EXTRA, 1, 0)
        load.wait()
        for dy in range(4):
            _, to_y, _ = target(0, 0, dy)
            cols = pl.ds(pl.multiple_of(to_y * QUARTER, QUARTER), QUARTER)
            packed = jnp.dot(pick_far, grads_ref[:, cols], preferred_element_type=jnp.float32).astype(jnp.bfloat16)
            if dy == 0:
                far[0, 0] = packed
            else:
                far_send[dy - 1] = packed
        pl.semaphore_wait(barrier, PEERS)
        for p in range(3):
            for dy in range(4):
                if p + dy:
                    far_copy(p, dy).start()
    else:
        load.wait()
        pl.semaphore_wait(barrier, PEERS)

    def pack(b, _):
        if main:
            pl.when(b == 2)(forward)
        picks = []
        slot = lax.broadcasted_iota(jnp.int32, (cap, ROWS), 0)
        for i in range(4):
            _, _, to_shard = target(b, i, 0)
            pick = jnp.where(rank[pl.ds(to_shard, 1), :] == slot, 1.0, 0.0).astype(jnp.bfloat16)
            send_ids[b * 4 + i, :, 0:cap] = ids_by(pick) - to_shard * VSH
            picks.append(pick)
        picks = jnp.concatenate(picks, axis=0)
        for dy in range(4):
            _, to_y, _ = target(b, 0, dy)
            cols = pl.ds(pl.multiple_of(to_y * QUARTER, QUARTER), QUARTER)
            packed = jnp.dot(picks, grads_ref[:, cols], preferred_element_type=jnp.float32).astype(jnp.bfloat16)
            for i in range(4):
                send[b * 16 + i * 4 + dy] = packed[i * cap : (i + 1) * cap]
                if i == 0 and dy == 0:

                    @pl.when(b == 0)
                    def _():
                        own_rows.start()
                        own_ids.start()

                    @pl.when(b > 0)
                    def _():
                        ids_copy(b, 0, 0).start()
                        rows_copy(b, 0, 0).start()
                else:
                    ids_copy(b, i, dy).start()
                    rows_copy(b, i, dy).start()
        return 0

    def sent():
        for b in range(BATCHES):
            settle(send, b * 16 + (b == 0), 16 - (b == 0), ssem.at[b])
            settle(recv_ids, b * 16 + (b == 0), 16 - (b == 0), isem.at[b])
        if main:
            settle(far.at[0], 1, 11, fs)
            for k in range(len(HOPS)):
                far_hop(k).wait_send()
            for part in range(2):
                for dx in (1, 2, 3):
                    onward(part, dx).wait_send()

    def add(block, t, ids, fresh=False):
        start = pl.multiple_of(t * CHUNK, 16)
        row = lax.broadcasted_iota(jnp.int32, (CHUNK, block.shape[0]), 0)
        hit = jnp.where(row == ids - start, 1.0, 0.0).astype(jnp.bfloat16)
        part = jnp.dot(hit, block, preferred_element_type=jnp.float32)
        rows = pl.ds(start, CHUNK)
        if fresh:
            acc[0, rows] = part[:, :HALF]
            acc[1, rows] = part[:, HALF:]
        else:
            acc[0, rows] += part[:, :HALF]
            acc[1, rows] += part[:, HALF:]

    def rows_of(b, start=0, stop=16):
        return recv[pl.ds(b * 16 + start, stop - start)].reshape((stop - start) * cap, QUARTER)

    def arrive(b):
        settle(recv, b * 16, 16, rsem.at[b])
        settle(recv_ids, b * 16, 16, jsem.at[b])

    def ids_of(b, start=0, stop=16):
        return jnp.concatenate([recv_ids[b * 16 + k][:, 0:cap] for k in range(start, stop)], axis=1)

    def exchange(t):
        rows = pl.ds(pl.multiple_of(t * CHUNK, 16), CHUNK)
        return pltpu.make_async_remote_copy(
            acc.at[1 - c, rows], other.at[rows], psem.at[t], qsem.at[t], device_id=partner, device_id_type=MESH
        )

    def sweep(block, ids, fresh=False, then=None):
        def step(t, ids):
            add(block(), t, ids, fresh)
            if then is not None:
                then(t)
            return ids

        lax.fori_loop(0, CHUNKS, step, ids)

    def batch(b, _):
        arrive(b)
        sweep(lambda: rows_of(b), ids_of(b))
        return 0

    def far_block(dx):
        at = [dx * 32 + r % 2 * 16 + r // 2 * 4 + dy for r in ORDER for dy in range(4)]
        ids = [recv_ids[j][:, cap : cap + EXTRA] for j in at]
        ids = jnp.concatenate(ids, axis=1) - shard * VSH
        sweep(lambda: far[dx].reshape(BLOCKS * EXTRA, QUARTER), ids)

    lax.fori_loop(0, BATCHES, pack, 0)
    own_rows.wait()
    own_ids.wait()
    settle(recv, 1, 15, rsem.at[0])
    settle(recv_ids, 1, 15, jsem.at[0])
    sweep(lambda: rows_of(0), ids_of(0), fresh=True)
    if main:
        for k in range(len(HOPS)):
            far_hop(k).wait_recv()
        for dx in (1, 2, 3):
            onward(1, dx).start()
        batch(1, 0)
        far_block(0)
        for dx in (1, 2, 3):
            lax.fori_loop(2 * dx, 2 * dx + 2 if dx < 3 else 7, batch, 0)
            for part in range(2):
                onward(part, dx).wait_recv()
            if dx == 3:
                settle(recv_ids, 112, 16, jsem.at[7])
            far_block(dx)
        worst = functools.reduce(jnp.maximum, [recv_ids[j][:, 127:128] for j in range(PEERS)])
        mark = jnp.broadcast_to(worst.astype(jnp.float32), (8, HALF))

        def then(t):
            @pl.when(t == CHUNKS - 1)
            def _():
                acc[1 - c, VSH : VSH + 8] = mark

            exchange(t).start()

        settle(recv, 112, 8, rsem.at[7])
        sweep(lambda: rows_of(7, stop=8), ids_of(7, stop=8))
        sent()
        settle(recv, 120, 8, rsem.at[8])
        sweep(lambda: rows_of(7, start=8), ids_of(7, start=8), then=then)
    else:
        lax.fori_loop(1, 7, batch, 0)
        settle(recv_ids, 112, 16, jsem.at[7])
        settle(recv, 112, 8, rsem.at[7])
        settle(recv, 120, 8, rsem.at[8])
        sent()
        sweep(lambda: rows_of(7), ids_of(7), then=lambda t: exchange(t).start())

    stores = []
    for t in range(CHUNKS):
        exchange(t).wait()
        a, n = t * CHUNK, min(CHUNK, VSH - t * CHUNK)
        if main and t == CHUNKS - 1:
            flag_ref[0] = jnp.max(jnp.maximum(mark, other[VSH : VSH + 8])).astype(jnp.int32)
        result = acc[c, a : a + n] + other[a : a + n]
        other[a : a + n] = result if main else sum_ref[a : a + n] + result
        stores.append(pltpu.make_async_copy(other.at[pl.ds(a, n)], out_hbm.at[pl.ds(a, n)], osem.at[t]))
        stores[t].start()
    for store in stores:
        store.wait()


def call(main, cap, *operands):
    shape = jax.ShapeDtypeStruct((VSH, HALF), jnp.float32)
    dma = pltpu.SemaphoreType.DMA
    scratch = [
        pltpu.VMEM((ROWS, 4 * QUARTER), jnp.bfloat16),
        dma,
        pltpu.VMEM((SHARDS, ROWS), jnp.int32),
        pltpu.VMEM((8, ROWS), jnp.int32),
        pltpu.VMEM((16, ROWS), jnp.bfloat16),
        pltpu.VMEM((PEERS, cap, QUARTER), jnp.bfloat16),
        pltpu.VMEM((SHARDS, 1, 128), jnp.int32),
        pltpu.VMEM((PEERS, cap, QUARTER), jnp.bfloat16),
        pltpu.VMEM((PEERS, 1, 128), jnp.int32),
        pltpu.VMEM((2, CHUNK * CHUNKS, HALF), jnp.float32),
        pltpu.VMEM((CHUNK * CHUNKS, HALF), jnp.float32),
    ] + [dma((BATCHES + 1,))] * 4 + [dma((CHUNKS,))] * 3 + [dma((2,))]
    if main:
        scratch += [
            pltpu.VMEM((3, EXTRA, QUARTER), jnp.bfloat16),
            pltpu.VMEM((4, BLOCKS, EXTRA, QUARTER), jnp.bfloat16),
        ] + [dma] * 2 + [dma((6,))] * 4
    whole = pl.BlockSpec(memory_space=pl.ANY)
    return pl.pallas_call(
        functools.partial(kernel, main, cap),
        out_shape=(shape, jax.ShapeDtypeStruct((1,), jnp.int32)) if main else shape,
        in_specs=[whole if k == 1 else pl.BlockSpec(memory_space=pltpu.VMEM) for k in range(len(operands))],
        out_specs=[whole, pl.BlockSpec(memory_space=pltpu.SMEM)] if main else whole,
        scratch_shapes=scratch,
        compiler_params=pltpu.CompilerParams(
            collective_id=0 if main else 1, has_side_effects=True, vmem_limit_bytes=56 << 20
        ),
        name="direct_rows" if main else "rest_rows",
    )(*operands)


def body(token_grads, token_ids):
    ids = token_ids.reshape(1, ROWS)
    sums, flag = call(True, DIRECT, ids, token_grads)
    return lax.cond(
        flag[0] > 0,
        lambda ids, grads, sums: call(False, REST, ids, grads, sums),
        lambda ids, grads, sums: sums,
        ids,
        token_grads,
        sums,
    )


def solution(mesh):
    return jax.shard_map(
        body,
        mesh=mesh,
        in_specs=(P(("dp", "vocab"), None), P(("dp", "vocab"))),
        out_specs=P("vocab", "dp"),
        check_vma=False,
    )
```

```python
import functools

import jax
import jax.numpy as jnp
from jax import lax
from jax.experimental import pallas as pl
from jax.experimental.pallas import tpu as pltpu
from jax.sharding import PartitionSpec as P

MESH = pl.DeviceIdType.MESH
VSH = 3912
SHARDS = 32
ROWS = 2048
DIRECT = 64
REST = 32
EXTRA = 32
CHUNK = 784
CHUNKS = 5
QUARTER = 256
HALF = 128
BATCHES = 8
PEERS = 128
BLOCKS = 32
ORDER = (0, 3, 5, 1, 6, 4, 7, 2)
HOPS = ((0, 1, 1), (5, 6, 1), (3, 4, 1), (0, 7, 7), (3, 2, 7), (5, 4, 7))


def place():
    dp, vocab = lax.axis_index("dp"), lax.axis_index("vocab")
    return dp // 2, dp % 2, vocab // 4, vocab % 4


def offset(b, i):
    return 2 * i + b % 2, b // 2


def target(b, i, dy):
    y, c, z, x = place()
    dz, dx = offset(b, i)
    to_z, to_x, to_y = (z + dz) % 8, (x + dx) % 4, (y + dy) % 4
    return (to_y * 2 + c, to_z * 4 + to_x), to_y, to_z * 4 + to_x


def running(marks, before, carry):
    count = jnp.dot(marks.astype(jnp.bfloat16), before, preferred_element_type=jnp.float32) + carry
    return count, carry + jnp.sum(marks, axis=1, keepdims=True)


def rank_rows(ids_ref, rank, extra, parts):
    ids = ids_ref[...]
    first = lax.broadcasted_iota(jnp.int32, (SHARDS, 1), 0) * VSH
    local = ids - first
    marks = jnp.where((local >= 0) & (local < VSH), 1.0, 0.0)
    row = lax.broadcasted_iota(jnp.int32, (16, ROWS), 0)
    split = jnp.where(row == 0, ids >> 12, jnp.where(row == 1, (ids >> 6) & 63, jnp.where(row == 2, ids & 63, 0)))
    parts[...] = split.astype(jnp.float32).astype(jnp.bfloat16)
    block = 256
    before = lax.broadcasted_iota(jnp.int32, (block, block), 0) < lax.broadcasted_iota(jnp.int32, (block, block), 1)
    before = jnp.where(before, 1.0, 0.0).astype(jnp.bfloat16)
    carry = jnp.zeros((SHARDS, 1), jnp.float32)
    total = jnp.zeros((16, 1), jnp.float32)
    for k in range(ROWS // block):
        m = marks[:, k * block : (k + 1) * block]
        count, carry = running(m, before, carry)
        count = jnp.where(m > 0.5, count, -1.0)
        rank[:, k * block : (k + 1) * block] = count.astype(jnp.int32)
        over = jnp.sum(jnp.where(count >= DIRECT, 1.0, 0.0), axis=0, keepdims=True)
        over = jnp.broadcast_to(over, (16, block))
        place_of, total = running(over, before, total)
        place_of = jnp.where(over > 0.5, place_of, -1.0).astype(jnp.int32)
        extra[:, k * block : (k + 1) * block] = place_of[0:8]
    return total[0:1]


def kernel(main, cap, *refs):
    if main:
        (ids_ref, grads_hbm, out_hbm, flag_ref), refs = refs[:4], refs[4:]
    else:
        (ids_ref, grads_hbm, sum_ref, out_hbm), refs = refs[:4], refs[4:]
    grads_ref, lsem, rank, extra, parts, send, send_ids, recv, recv_ids, acc, other, ssem, isem, rsem, jsem, psem, qsem, osem, own = refs[:19]
    if main:
        far_send, far, fs, fr, zs, zr, gs, gr = refs[19:]
    y, c, z, x = place()
    partner = (y * 2 + 1 - c, z * 4 + x)
    shard = z * 4 + x
    barrier = pltpu.get_barrier_semaphore()

    load = pltpu.make_async_copy(grads_hbm, grads_ref, lsem)
    load.start()
    planes = [(z + dz) % 8 * 4 for dz in range(8)]
    lines = [(x + dx) % 4 for dx in range(4)]
    groups = [(y + dy) % 4 * 2 + c for dy in range(4)]
    for j in range(1, PEERS):
        dz, dx, dy = j // 16, j // 4 % 4, j % 4
        peer = (groups[dy], planes[dz] + lines[dx])
        pl.semaphore_signal(barrier, inc=1, device_id=peer, device_id_type=MESH)
    pl.semaphore_signal(barrier, inc=1, device_id=partner, device_id_type=MESH)
    total = rank_rows(ids_ref, rank, extra, parts)
    send_ids[...] = jnp.zeros_like(send_ids)
    if main:
        spare = jnp.where(extra[0:1, :] >= 0, extra[0:1, :], EXTRA)
        pick_far = jnp.where(spare == lax.broadcasted_iota(jnp.int32, (EXTRA, ROWS), 0), 1.0, 0.0).astype(jnp.bfloat16)
    else:
        late = extra[0:1, :] >= EXTRA
        rank[...] = jnp.where(late & (rank[...] >= DIRECT), rank[...] - DIRECT, -1)
    def slot_of(b, i):
        return b + jnp.where(b == BATCHES - 1, i // 2, 0)

    def settle(ref, start, count, sem):
        span = ref.at[pl.ds(start, count)]
        pltpu.make_async_copy(span, span, sem).wait()

    def rows_copy(b, i, dy):
        peer, _, _ = target(b, i, dy)
        j = b * 16 + i * 4 + dy
        return pltpu.make_async_remote_copy(send.at[j], recv.at[j], ssem.at[b], rsem.at[slot_of(b, i)], device_id=peer, device_id_type=MESH)

    def ids_copy(b, i, dy):
        peer, _, _ = target(b, i, dy)
        j = b * 16 + i * 4 + dy
        return pltpu.make_async_remote_copy(
            send_ids.at[b * 4 + i], recv_ids.at[j], isem.at[b], jsem.at[b], device_id=peer, device_id_type=MESH
        )

    def far_copy(p, dy):
        source = far_send.at[dy - 1] if dy else far.at[0, 0]
        peer = ((y + dy) % 4 * 2 + c, (z + ORDER[p]) % 8 * 4 + x)
        return pltpu.make_async_remote_copy(source, far.at[0, p * 4 + dy], fs, fr, device_id=peer, device_id_type=MESH)

    def far_hop(k):
        took, gives, dz = HOPS[k]
        first, count = (0, 4) if gives != 4 else (0, 2) if dz == 1 else (2, 2)
        return pltpu.make_async_remote_copy(
            far.at[0, pl.ds(ORDER.index(took) * 4 + first, count)],
            far.at[0, pl.ds(ORDER.index(gives) * 4 + first, count)],
            zs.at[k],
            zr.at[k],
            device_id=(y * 2 + c, (z + dz) % 8 * 4 + x),
            device_id_type=MESH,
        )

    def onward(part, dx):
        span = pl.ds(0, 12) if part == 0 else pl.ds(12, 20)
        s = part * 3 + dx - 1
        return pltpu.make_async_remote_copy(
            far.at[0, span],
            far.at[dx, span],
            gs.at[s],
            gr.at[s],
            device_id=(y * 2 + c, z * 4 + (x + dx) % 4),
            device_id_type=MESH,
        )

    def forward():
        settle(far.at[0], 1, 11, fr)
        for k in range(len(HOPS)):
            far_hop(k).start()
        for dx in (1, 2, 3):
            onward(0, dx).start()

    own_rows = pltpu.make_async_copy(send.at[0], recv.at[0], own.at[0])
    own_ids = pltpu.make_async_copy(send_ids.at[0], recv_ids.at[0], own.at[1])

    def ids_by(pick):
        three = lax.dot_general(parts[...], pick, (((1,), (1,)), ((), ())), preferred_element_type=jnp.float32)
        return (three[0:1] * 4096.0 + three[1:2] * 64.0 + three[2:3]).astype(jnp.int32)

    if main:
        far_ids = ids_by(pick_far)
        for k in range(SHARDS):
            send_ids[k, :, cap : cap + EXTRA] = far_ids
            send_ids[k, :, 127:128] = jnp.where(total > EXTRA, 1, 0)
        load.wait()
        for dy in range(4):
            _, to_y, _ = target(0, 0, dy)
            cols = pl.ds(pl.multiple_of(to_y * QUARTER, QUARTER), QUARTER)
            packed = jnp.dot(pick_far, grads_ref[:, cols], preferred_element_type=jnp.float32).astype(jnp.bfloat16)
            if dy == 0:
                far[0, 0] = packed
            else:
                far_send[dy - 1] = packed
        pl.semaphore_wait(barrier, PEERS)
        for p in range(3):
            for dy in range(4):
                if p + dy:
                    far_copy(p, dy).start()
    else:
        load.wait()
        pl.semaphore_wait(barrier, PEERS)

    def pack(b, _):
        if main:
            pl.when(b == 1)(forward)
        picks = []
        slot = lax.broadcasted_iota(jnp.int32, (cap, ROWS), 0)
        for i in range(4):
            _, _, to_shard = target(b, i, 0)
            pick = jnp.where(rank[pl.ds(to_shard, 1), :] == slot, 1.0, 0.0).astype(jnp.bfloat16)
            send_ids[b * 4 + i, :, 0:cap] = ids_by(pick) - to_shard * VSH
            picks.append(pick)
        picks = jnp.concatenate(picks, axis=0)
        for dy in range(4):
            _, to_y, _ = target(b, 0, dy)
            cols = pl.ds(pl.multiple_of(to_y * QUARTER, QUARTER), QUARTER)
            packed = jnp.dot(picks, grads_ref[:, cols], preferred_element_type=jnp.float32).astype(jnp.bfloat16)
            for i in range(4):
                send[b * 16 + i * 4 + dy] = packed[i * cap : (i + 1) * cap]
                if i == 0 and dy == 0:

                    @pl.when(b == 0)
                    def _():
                        own_rows.start()
                        own_ids.start()

                    @pl.when(b > 0)
                    def _():
                        ids_copy(b, 0, 0).start()
                        rows_copy(b, 0, 0).start()
                else:
                    ids_copy(b, i, dy).start()
                    rows_copy(b, i, dy).start()
        return 0

    def sent():
        for b in range(BATCHES):
            settle(send, b * 16 + (b == 0), 16 - (b == 0), ssem.at[b])
            settle(recv_ids, b * 16 + (b == 0), 16 - (b == 0), isem.at[b])
        if main:
            settle(far.at[0], 1, 11, fs)
            for k in range(len(HOPS)):
                far_hop(k).wait_send()
            for part in range(2):
                for dx in (1, 2, 3):
                    onward(part, dx).wait_send()

    def add(block, t, ids, fresh=False):
        start = pl.multiple_of(t * CHUNK, 16)
        row = lax.broadcasted_iota(jnp.int32, (CHUNK, block.shape[0]), 0)
        hit = jnp.where(row == ids - start, 1.0, 0.0).astype(jnp.bfloat16)
        part = jnp.dot(hit, block, preferred_element_type=jnp.float32)
        rows = pl.ds(start, CHUNK)
        if fresh:
            acc[0, rows] = part[:, :HALF]
            acc[1, rows] = part[:, HALF:]
        else:
            acc[0, rows] += part[:, :HALF]
            acc[1, rows] += part[:, HALF:]

    def rows_of(b, start=0, stop=16):
        return recv[pl.ds(b * 16 + start, stop - start)].reshape((stop - start) * cap, QUARTER)

    def arrive(b):
        settle(recv, b * 16, 16, rsem.at[b])
        settle(recv_ids, b * 16, 16, jsem.at[b])

    def ids_of(b, start=0, stop=16):
        return jnp.concatenate([recv_ids[b * 16 + k][:, 0:cap] for k in range(start, stop)], axis=1)

    def exchange(t):
        rows = pl.ds(pl.multiple_of(t * CHUNK, 16), CHUNK)
        return pltpu.make_async_remote_copy(
            acc.at[1 - c, rows], other.at[rows], psem.at[t], qsem.at[t], device_id=partner, device_id_type=MESH
        )

    def sweep(block, ids, fresh=False, then=None):
        def step(t, ids):
            add(block(), t, ids, fresh)
            if then is not None:
                then(t)
            return ids

        lax.fori_loop(0, CHUNKS, step, ids)

    def batch(b, _):
        arrive(b)
        sweep(lambda: rows_of(b), ids_of(b))
        return 0

    def far_block(dx):
        at = [dx * 32 + r % 2 * 16 + r // 2 * 4 + dy for r in ORDER for dy in range(4)]
        ids = [recv_ids[j][:, cap : cap + EXTRA] for j in at]
        ids = jnp.concatenate(ids, axis=1) - shard * VSH
        sweep(lambda: far[dx].reshape(BLOCKS * EXTRA, QUARTER), ids)

    lax.fori_loop(0, BATCHES, pack, 0)
    own_rows.wait()
    own_ids.wait()
    settle(recv, 1, 15, rsem.at[0])
    settle(recv_ids, 1, 15, jsem.at[0])
    sweep(lambda: rows_of(0), ids_of(0), fresh=True)
    if main:
        for k in range(len(HOPS)):
            far_hop(k).wait_recv()
        for dx in (1, 2, 3):
            onward(1, dx).start()
        batch(1, 0)
        far_block(0)
        for dx in (1, 2, 3):
            lax.fori_loop(2 * dx, 2 * dx + 2 if dx < 3 else 7, batch, 0)
            for part in range(2):
                onward(part, dx).wait_recv()
            if dx == 3:
                settle(recv_ids, 112, 16, jsem.at[7])
            far_block(dx)
        worst = functools.reduce(jnp.maximum, [recv_ids[j][:, 127:128] for j in range(PEERS)])
        mark = jnp.broadcast_to(worst.astype(jnp.float32), (8, HALF))

        def then(t):
            @pl.when(t == CHUNKS - 1)
            def _():
                acc[1 - c, VSH : VSH + 8] = mark

            exchange(t).start()

        settle(recv, 112, 8, rsem.at[7])
        sweep(lambda: rows_of(7, stop=8), ids_of(7, stop=8))
        settle(recv, 120, 8, rsem.at[8])
        sweep(lambda: rows_of(7, start=8), ids_of(7, start=8), then=then)
    else:
        lax.fori_loop(1, 7, batch, 0)
        settle(recv_ids, 112, 16, jsem.at[7])
        settle(recv, 112, 8, rsem.at[7])
        settle(recv, 120, 8, rsem.at[8])
        sent()
        sweep(lambda: rows_of(7), ids_of(7), then=lambda t: exchange(t).start())

    stores = []
    for t in range(CHUNKS):
        exchange(t).wait()
        a, n = t * CHUNK, min(CHUNK, VSH - t * CHUNK)
        if main and t == CHUNKS - 1:
            flag_ref[0] = jnp.max(jnp.maximum(mark, other[VSH : VSH + 8])).astype(jnp.int32)
        result = acc[c, a : a + n] + other[a : a + n]
        other[a : a + n] = result if main else sum_ref[a : a + n] + result
        stores.append(pltpu.make_async_copy(other.at[pl.ds(a, n)], out_hbm.at[pl.ds(a, n)], osem.at[t]))
        stores[t].start()
    if main:
        sent()
    for store in stores:
        store.wait()


def call(main, cap, *operands):
    shape = jax.ShapeDtypeStruct((VSH, HALF), jnp.float32)
    dma = pltpu.SemaphoreType.DMA
    scratch = [
        pltpu.VMEM((ROWS, 4 * QUARTER), jnp.bfloat16),
        dma,
        pltpu.VMEM((SHARDS, ROWS), jnp.int32),
        pltpu.VMEM((8, ROWS), jnp.int32),
        pltpu.VMEM((16, ROWS), jnp.bfloat16),
        pltpu.VMEM((PEERS, cap, QUARTER), jnp.bfloat16),
        pltpu.VMEM((SHARDS, 1, 128), jnp.int32),
        pltpu.VMEM((PEERS, cap, QUARTER), jnp.bfloat16),
        pltpu.VMEM((PEERS, 1, 128), jnp.int32),
        pltpu.VMEM((2, CHUNK * CHUNKS, HALF), jnp.float32),
        pltpu.VMEM((CHUNK * CHUNKS, HALF), jnp.float32),
    ] + [dma((BATCHES + 1,))] * 4 + [dma((CHUNKS,))] * 3 + [dma((2,))]
    if main:
        scratch += [
            pltpu.VMEM((3, EXTRA, QUARTER), jnp.bfloat16),
            pltpu.VMEM((4, BLOCKS, EXTRA, QUARTER), jnp.bfloat16),
        ] + [dma] * 2 + [dma((6,))] * 4
    whole = pl.BlockSpec(memory_space=pl.ANY)
    return pl.pallas_call(
        functools.partial(kernel, main, cap),
        out_shape=(shape, jax.ShapeDtypeStruct((1,), jnp.int32)) if main else shape,
        in_specs=[whole if k == 1 else pl.BlockSpec(memory_space=pltpu.VMEM) for k in range(len(operands))],
        out_specs=[whole, pl.BlockSpec(memory_space=pltpu.SMEM)] if main else whole,
        scratch_shapes=scratch,
        compiler_params=pltpu.CompilerParams(
            collective_id=0 if main else 1, has_side_effects=True, vmem_limit_bytes=56 << 20
        ),
        name="direct_rows" if main else "rest_rows",
    )(*operands)


def body(token_grads, token_ids):
    ids = token_ids.reshape(1, ROWS)
    sums, flag = call(True, DIRECT, ids, token_grads)
    return lax.cond(
        flag[0] > 0,
        lambda ids, grads, sums: call(False, REST, ids, grads, sums),
        lambda ids, grads, sums: sums,
        ids,
        token_grads,
        sums,
    )


def solution(mesh):
    return jax.shard_map(
        body,
        mesh=mesh,
        in_specs=(P(("dp", "vocab"), None), P(("dp", "vocab"))),
        out_specs=P("vocab", "dp"),
        check_vma=False,
    )
```
